512 devices in a mesh: row: 8 (over y, core), col: 64 (over x, z).
Axes of the slice: x: 4, y: 4, z: 16, core: 2. Of those that a mesh axis runs over, the one named last changes fastest.
Arguments:
- matrix: bfloat16 [8192, 8192], P('row', 'col'), may hold values from -6 to 6
- lower_inverse: bfloat16 [2, 1024, 1024], P(None, 'row'), may hold values from -0.03125 to 0.03125
- upper_inverse: bfloat16 [2, 1024, 1024], P(None, 'row'), may hold values from -0.03125 to 0.03125
Outputs:
- factored: bfloat16 [8192, 8192], P('row', 'col')
The draws below stay inside these ranges and needn't reach their ends.
All inputs are finite; a program needn't handle non-finite values.
Results may differ from the reference program's by a relative error of at most 0.013.
Values may be sent and summed in bfloat16 or wider, within the bound.
No kernel may reach another device: no remote copies, remote signals or barrier semaphores. Data moves between devices by JAX's collectives and lax.ppermute only.
A program may use at most 64 MiB of HBM per device.

```python
import jax
import jax.numpy as jnp
from jax import lax

NB = 1024
STEPS = 2
ORDER = 8192


def level_of(rng, extent, cuts, least, largest):
    gain = 1.0
    for dim, blocks in cuts:
        heights = jax.random.uniform(jax.random.fold_in(jax.random.fold_in(rng, 6), dim), (blocks,), jnp.float32, least / len(cuts), largest / len(cuts))
        gain = gain * jnp.repeat(jnp.exp(heights), extent[dim] // blocks).reshape((-1,) + (1,) * (len(extent) - 1 - dim))
    return gain


def centred(own_key, extent, width, most, pieces=(), held_as=jnp.bfloat16):
    array = jax.random.normal(own_key, extent, jnp.float32) * width
    if len(pieces) > 0:
        array = level_of(own_key, extent, pieces, -0.22, 0.18) * array
    return jnp.clip(array, min=-most, max=most).astype(held_as)


def setup_inputs(seed: int = 0) -> dict:
    streams_of = jax.random.split(jax.random.key(seed), 4)
    return {
        "matrix": centred(streams_of[0], (ORDER, ORDER), 1.0, 6.0, ((0, 8), (1, 64))),
        "lower_inverse": centred(streams_of[1], (STEPS, NB, NB), (32 * NB) ** -0.5, 0.03125, ((1, 8),)),
        "upper_inverse": centred(streams_of[2], (STEPS, NB, NB), (32 * NB) ** -0.5, 0.03125, ((1, 8),)),
    }


def reference(matrix, lower_inverse, upper_inverse):
    working = matrix
    for step_index in range(STEPS):
        block_low = step_index * NB
        block_high = block_low + NB
        left_panel = working[block_high:, block_low:block_high]
        column_factor = jnp.dot(left_panel, upper_inverse[step_index], preferred_element_type=jnp.float32).astype(jnp.bfloat16)
        row_factor = jnp.dot(lower_inverse[step_index], working[block_low:block_high, block_high:], preferred_element_type=jnp.float32).astype(jnp.bfloat16)
        coupling = jnp.dot(upper_inverse[step_index], row_factor, preferred_element_type=jnp.float32).astype(jnp.bfloat16)
        trail_part = working[block_high:, block_high:]
        height = trail_part.shape[0]
        blocks = trail_part.shape[1] // NB
        trail_blocks = trail_part.reshape(height, blocks, NB).transpose(1, 0, 2)
        coupling_blocks = coupling.reshape(NB, blocks, NB).transpose(1, 0, 2)

        def update(operands):
            old_block, right_block = operands
            product = jnp.dot(left_panel, right_block, preferred_element_type=jnp.float32)
            return (old_block.astype(jnp.float32) - product).astype(jnp.bfloat16)

        updated = lax.map(update, (trail_blocks, coupling_blocks))
        updated = updated.transpose(1, 0, 2).reshape(height, blocks * NB)
        working = working.at[block_high:, block_low:block_high].set(column_factor)
        working = working.at[block_low:block_high, block_high:].set(row_factor)
        working = working.at[block_high:, block_high:].set(updated)
    return working
```

```python
import jax
import jax.numpy as jnp
from jax import lax
from jax.sharding import Mesh, PartitionSpec as P

NB = 1024
BF = jnp.bfloat16
F32 = jnp.float32


def dot(a, b):
    return jnp.dot(a, b, preferred_element_type=F32)


def from_first(value, axis, count):
    at = lax.axis_index(axis)
    got = [lax.ppermute(value, axis, [(0, k)]) for k in range(1, count)]
    out = value
    for k in range(1, count):
        out = jnp.where(at == k, got[k - 1], out)
    return out


def both(half):
    n = half.shape[-1]
    whole = lax.all_gather(half.reshape(4, 128, n), "core", axis=1)
    return whole.reshape(1024, n)


def spread_to_all(piece, axis, count):
    copies = jnp.broadcast_to(piece[None], (count,) + piece.shape)
    return lax.all_to_all(copies, axis, 0, 0)


def shards(a, lower, upper):
    y = lax.axis_index("y")
    core = lax.axis_index("core")
    x = lax.axis_index("x")
    z = lax.axis_index("z")
    j = x * 16 + z
    in0 = j < 8
    in1 = (j >= 8) & (j < 16)
    start0 = jnp.clip(j * 128, 0, NB - 128)
    start1 = jnp.clip(j * 128 - NB, 0, NB - 128)

    piece = from_first(a, "x", 4)
    panel = lax.all_gather(piece, "z", axis=0)

    packed = jnp.concatenate([lower, upper], axis=0)
    halves = lax.all_gather(packed, "y", axis=0)
    l0, l1, u0, u1 = (halves[:, m].reshape(512, NB) for m in range(4))

    pieces = lax.all_gather(piece, "core", axis=0)
    off = jnp.where(z < 8, pieces[1], pieces[0]).reshape(4, 2, 128, 128)
    mine = lax.dynamic_slice(off, (x, core, 0, 0), (1, 1, 128, 128)).reshape(128, 128)
    off_z = spread_to_all(mine, "z", 16)
    off_all = spread_to_all(off_z, "x", 4)
    a10 = off_all[:, :8].transpose(0, 2, 1, 3).reshape(512, NB)
    a01 = off_all[:, 8:].transpose(0, 2, 1, 3).reshape(512, NB)

    tops = lax.all_gather(a, "core", axis=0)
    top0, top1 = tops[0], tops[1]
    mine1 = lax.dynamic_slice_in_dim(top1.reshape(4, 2, 128, 128), core, 1, 1).reshape(512, 128)
    r0 = both(dot(l0, top0).astype(BF))
    c0_half = dot(u0, r0).astype(BF)
    u0_cols = lax.dynamic_slice_in_dim(u0, start0, 128, 1)
    c0_half = jnp.where(in0, -u0_cols, c0_half)
    c0 = both(c0_half)
    w1 = both((mine1.astype(F32) - dot(a10, c0)).astype(BF))
    r1 = both(dot(l1, w1).astype(BF))
    c1_half = dot(u1, r1).astype(BF)
    u1_cols = lax.dynamic_slice_in_dim(u1, start1, 128, 1)
    c1_half = jnp.where(in0, jnp.zeros_like(c1_half), jnp.where(in1, -u1_cols, c1_half))
    c1 = both(c1_half)
    t = both(dot(a01, c1).astype(BF))
    s = both(dot(l0, t).astype(BF))
    base = jnp.where(in1, jnp.zeros_like(c0_half), c0_half).astype(F32)
    d_half = (base - dot(u0, s)).astype(BF)

    pair = jnp.concatenate([d_half.reshape(4, 128, 128), c1_half.reshape(4, 128, 128)], axis=0)
    pair = from_first(pair, "y", 4)
    right = lax.all_gather(pair, "core", axis=1).reshape(16, 128, 128)

    product = lax.dot_general(
        panel, right, (((0, 2), (0, 1)), ((), ())), preferred_element_type=F32
    )
    trail = (jnp.where(j >= 16, a, jnp.zeros_like(a)).astype(F32) - product).astype(BF)
    row0 = jnp.where(in0, a, r0)
    row1 = jnp.where(in0, trail, jnp.where(in1, w1, r1))
    out = jnp.where(y > 0, trail, jnp.where(core == 0, row0, row1))
    return out


def solution(mesh):
    fine = Mesh(mesh.devices.reshape(4, 2, 4, 16), ("y", "core", "x", "z"))
    placed = (
        P(("y", "core"), ("x", "z")),
        P(None, ("y", "core"), None),
        P(None, ("y", "core"), None),
    )
    return jax.shard_map(
        shards, mesh=fine, in_specs=placed, out_specs=placed[0], check_vma=False
    )
```

```python
import jax
import jax.numpy as jnp
from jax import lax
from jax.sharding import Mesh, PartitionSpec as P

NB = 1024
BF = jnp.bfloat16
F32 = jnp.float32


def dot(a, b):
    return jnp.dot(a, b, preferred_element_type=F32)


def after(value, *others):
    return lax.optimization_barrier((value,) + others)[0]


def from_first(values, axis):
    at = lax.axis_index(axis)
    out = values[0]
    got = [lax.ppermute(v, axis, [(0, k)]) for k, v in enumerate(values) if k > 0]
    for k, v in enumerate(got):
        out = jnp.where(at == k + 1, v, out)
    return out


def copies(piece, count):
    return jnp.broadcast_to(piece[None], (count,) + piece.shape)


def cores(value):
    return lax.all_gather(value, "core", axis=0)


def shards(a, lower, upper):
    y = lax.axis_index("y")
    core = lax.axis_index("core")
    x = lax.axis_index("x")
    z = lax.axis_index("z")
    j = x * 16 + z
    in0 = j < 8
    in1 = (j >= 8) & (j < 16)
    zeros = jnp.zeros_like(a)

    panel = lax.all_gather(from_first([a] * 4, "x"), "z", axis=0)

    inverses = jnp.stack([lower, upper], axis=1)
    kept = lax.dynamic_index_in_dim(inverses, core, 0, False)
    given = lax.dynamic_index_in_dim(inverses, 1 - core, 0, False)
    taken = lax.ppermute(given, "core", [(0, 1), (1, 0)])
    pair = jnp.where(core == 0, jnp.stack([kept, taken], 1), jnp.stack([taken, kept], 1))
    parts = [pair] + [lax.ppermute(pair, "y", [(k, 0)]) for k in range(1, 4)]

    inv_l, inv_u = (jnp.concatenate([part[m].reshape(256, NB) for part in parts]) for m in range(2))
    inv_l, inv_u = lax.optimization_barrier((inv_l, inv_u))

    def times(inverse, right):
        return dot(inverse, right).astype(BF)

    r = times(inv_l, a)
    start = jnp.clip(j * 128 - core * NB, 0, NB - 128)
    u_cols = lax.dynamic_slice_in_dim(inv_u, start, 128, 1)
    c0 = jnp.where(in0, -u_cols, times(inv_u, r))
    c0 = cores(c0)[0]

    block = lax.dynamic_slice_in_dim(panel, 8 * (1 - core), 8, 0)

    def product(left, right):
        right = right.reshape(-1, 128, 128)
        return jnp.einsum("zrk,zkn->rn", left, right, preferred_element_type=F32)

    w = (jnp.where(in0, zeros, a).astype(F32) - product(block, c0)).astype(BF)
    r1 = times(inv_l, w)
    c1 = jnp.where(in0, zeros, jnp.where(in1, -u_cols, times(inv_u, r1)))
    c1 = cores(c1)[1]
    t = lax.optimization_barrier(product(block, c1).astype(BF))
    s = lax.optimization_barrier(times(inv_l, t))
    d = (jnp.where(in1, zeros, c0).astype(F32) - dot(inv_u, s)).astype(BF)
    right = jnp.where(core == 0, d, c1)
    right = from_first([right] * 4, "y")
    right = cores(right).reshape(2 * NB, 128)
    changed = product(panel, right)
    trail = (jnp.where(j >= 16, a, zeros).astype(F32) - changed).astype(BF)
    row0 = jnp.where(in0, a, r)
    row1 = jnp.where(j < 16, w, r1)
    return jnp.where(y > 0, trail, jnp.where(core == 0, row0, row1))


def solution(mesh):
    fine = Mesh(mesh.devices.reshape(4, 2, 4, 16), ("y", "core", "x", "z"))
    placed = (
        P(("y", "core"), ("x", "z")),
        P(None, ("y", "core"), None),
        P(None, ("y", "core"), None),
    )
    return jax.shard_map(
        shards, mesh=fine, in_specs=placed, out_specs=placed[0], check_vma=False
    )
```

```python
import jax
import jax.numpy as jnp
from jax import lax
from jax.sharding import Mesh, PartitionSpec as P

NB = 1024
BF = jnp.bfloat16
F32 = jnp.float32


def dot(a, b):
    return jnp.dot(a, b, preferred_element_type=F32)


def after(value, *others):
    return lax.optimization_barrier((value,) + others)[0]


def from_first(values, axis):
    at = lax.axis_index(axis)
    out = values[0]
    got = [lax.ppermute(v, axis, [(0, k)]) for k, v in enumerate(values) if k > 0]
    for k, v in enumerate(got):
        out = jnp.where(at == k + 1, v, out)
    return out


def copies(piece, count):
    return jnp.broadcast_to(piece[None], (count,) + piece.shape)


def cores(value):
    return lax.all_gather(value, "core", axis=0)


def shards(a, lower, upper):
    y = lax.axis_index("y")
    core = lax.axis_index("core")
    x = lax.axis_index("x")
    z = lax.axis_index("z")
    j = x * 16 + z
    in0 = j < 8
    in1 = (j >= 8) & (j < 16)
    zeros = jnp.zeros_like(a)

    share = from_first([a[256 * k : 256 * (k + 1)] for k in range(4)], "x")

    inverses = jnp.stack([lower, upper], axis=1)
    kept = lax.dynamic_index_in_dim(inverses, core, 0, False)
    given = lax.dynamic_index_in_dim(inverses, 1 - core, 0, False)
    taken = lax.ppermute(given, "core", [(0, 1), (1, 0)])
    pair = jnp.where(core == 0, jnp.stack([kept, taken], 1), jnp.stack([taken, kept], 1))
    pair = after(pair, share)
    parts = [pair] + [lax.ppermute(pair, "y", [(k, 0)]) for k in range(1, 4)]

    fours = [[k, k + 4, k + 8, k + 12] for k in range(4)]
    own = lax.all_to_all(copies(share, 4), "z", 0, 0, axis_index_groups=fours)

    def from_z(value, distance):
        return lax.ppermute(value, "z", [((k + distance) % 16, k) for k in range(16)])

    plus, minus = from_z(own, 1), from_z(own, -1)
    two = jnp.concatenate([from_z(own[:, :128], 2), from_z(own[:, 128:], -2)], axis=1)
    along = jnp.concatenate([own, plus, two, minus, own, plus, two])
    along = lax.dynamic_slice_in_dim(along, (4 - z % 4) % 4 * 4, 16, 0).reshape(4, 4, 256, 128)

    def half(which):
        blocks = lax.dynamic_slice_in_dim(along, 2 * which, 2, 1)
        return blocks.transpose(2, 1, 0, 3).reshape(256, NB)

    sent = copies(half(1 - core), 4)
    one = lax.all_to_all(sent, "x", 0, 0).reshape(NB, NB)
    sent_late = copies(half(core), 4)
    two = lax.all_to_all(sent_late, "x", 0, 0).reshape(NB, NB)

    parts = [after(part, sent) for part in parts]
    inv_l, inv_u = (jnp.concatenate([part[m].reshape(256, NB) for part in parts]) for m in range(2))
    inv_l, inv_u = lax.optimization_barrier((inv_l, inv_u))

    def times(inverse, right):
        return dot(inverse, right).astype(BF)

    r = times(inv_l, a)
    start = jnp.clip(j * 128 - core * NB, 0, NB - 128)
    u_cols = lax.dynamic_slice_in_dim(inv_u, start, 128, 1)
    c0 = jnp.where(in0, -u_cols, times(inv_u, r))
    c0 = after(c0, sent_late)
    c0 = cores(c0)[0]

    w = (jnp.where(in0, zeros, a).astype(F32) - dot(one, c0)).astype(BF)
    r1 = times(inv_l, w)
    c1 = jnp.where(in0, zeros, jnp.where(in1, -u_cols, times(inv_u, r1)))
    c1 = cores(c1)[1]
    t = lax.optimization_barrier(dot(one, c1).astype(BF))
    s = lax.optimization_barrier(times(inv_l, t))
    d = (jnp.where(in1, zeros, c0).astype(F32) - dot(inv_u, s)).astype(BF)
    right = jnp.where(core == 0, d, c1)
    right = from_first([right] * 4, "y")
    d, c1 = lax.optimization_barrier(tuple(cores(right)))
    changed = dot(one, jnp.where(core == 1, d, c1))
    changed += dot(two, jnp.where(core == 1, c1, d))
    trail = (jnp.where(j >= 16, a, zeros).astype(F32) - changed).astype(BF)
    row0 = jnp.where(in0, a, r)
    row1 = jnp.where(j < 16, w, r1)
    return jnp.where(y > 0, trail, jnp.where(core == 0, row0, row1))


def solution(mesh):
    fine = Mesh(mesh.devices.reshape(4, 2, 4, 16), ("y", "core", "x", "z"))
    placed = (
        P(("y", "core"), ("x", "z")),
        P(None, ("y", "core"), None),
        P(None, ("y", "core"), None),
    )
    return jax.shard_map(
        shards, mesh=fine, in_specs=placed, out_specs=placed[0], check_vma=False
    )
```

```python
import jax
import jax.numpy as jnp
from jax import lax
from jax.sharding import Mesh, PartitionSpec as P

NB = 1024
BF = jnp.bfloat16
F32 = jnp.float32


def dot(a, b):
    return jnp.dot(a, b, preferred_element_type=F32)


def after(value, *others):
    return lax.optimization_barrier((value,) + others)[0]


def from_first(values, axis):
    at = lax.axis_index(axis)
    out = values[0]
    got = [lax.ppermute(v, axis, [(0, k)]) for k, v in enumerate(values) if k > 0]
    for k, v in enumerate(got):
        out = jnp.where(at == k + 1, v, out)
    return out


def copies(piece, count):
    return jnp.broadcast_to(piece[None], (count,) + piece.shape)


def cores(value):
    return lax.all_gather(value, "core", axis=0)


def shards(a, lower, upper):
    y = lax.axis_index("y")
    core = lax.axis_index("core")
    x = lax.axis_index("x")
    z = lax.axis_index("z")
    j = x * 16 + z
    in0 = j < 8
    in1 = (j >= 8) & (j < 16)
    zeros = jnp.zeros_like(a)

    share = from_first([a[256 * k : 256 * (k + 1)] for k in range(4)], "x")

    inverses = jnp.stack([lower, upper], axis=1)
    kept = lax.dynamic_index_in_dim(inverses, core, 0, False)
    given = lax.dynamic_index_in_dim(inverses, 1 - core, 0, False)
    taken = lax.ppermute(given, "core", [(0, 1), (1, 0)])
    pair = jnp.where(core == 0, jnp.stack([kept, taken], 1), jnp.stack([taken, kept], 1))
    pair = after(pair, share)
    parts = [pair] + [lax.ppermute(pair, "y", [(k, 0)]) for k in range(1, 4)]

    fours = [[k, k + 4, k + 8, k + 12] for k in range(4)]
    own = lax.all_to_all(copies(share, 4), "z", 0, 0, axis_index_groups=fours)

    def from_z(value, distance):
        return lax.ppermute(value, "z", [((k + distance) % 16, k) for k in range(16)])

    plus, minus = from_z(own, 1), from_z(own, -1)
    two = lax.ppermute(own, "z", [((k + 2 - 4 * (k % 2)) % 16, k) for k in range(16)])
    along = jnp.concatenate([own, plus, two, minus, own, plus, two])
    along = lax.dynamic_slice_in_dim(along, (4 - z % 4) % 4 * 4, 16, 0).reshape(4, 4, 256, 128)

    def half(which):
        blocks = lax.dynamic_slice_in_dim(along, 2 * which, 2, 1)
        return blocks.transpose(1, 0, 2, 3).reshape(8, 256, 128)

    sent = copies(half(1 - core), 4)
    one = lax.all_to_all(sent, "x", 0, 0)

    inv_l, inv_u = (jnp.concatenate([part[m].reshape(256, NB) for part in parts]) for m in range(2))
    inv_l, inv_u = lax.optimization_barrier((inv_l, inv_u))

    def times(inverse, right):
        return dot(inverse, right).astype(BF)

    r = times(inv_l, a)
    start = jnp.clip(j * 128 - core * NB, 0, NB - 128)
    u_cols = lax.dynamic_slice_in_dim(inv_u, start, 128, 1)
    c0 = jnp.where(in0, -u_cols, times(inv_u, r))
    sent_late = after(half(core), r).transpose(1, 0, 2).reshape(256, NB)
    sent_late = copies(sent_late, 4)
    two = lax.all_to_all(sent_late, "x", 0, 0).reshape(NB, NB)
    c0 = after(c0, sent_late)
    c0x = lax.ppermute(c0, ("y", "core"), [(0, 1)])

    def product(left, right):
        right = right.reshape(8, 128, 128)
        return jnp.einsum("xzrk,zkn->xrn", left, right, preferred_element_type=F32).reshape(NB, 128)

    w = (jnp.where(in0, zeros, a).astype(F32) - product(one, c0x)).astype(BF)
    r1 = times(inv_l, w)
    c1 = jnp.where(in0, zeros, jnp.where(in1, -u_cols, times(inv_u, r1)))
    c1 = cores(c1)[1]
    t = lax.optimization_barrier(product(one, c1).astype(BF))
    s = lax.optimization_barrier(times(inv_l, t))
    d = (jnp.where(in1, zeros, c0).astype(F32) - dot(inv_u, s)).astype(BF)
    right = jnp.where(core == 0, d, c1)
    right = from_first([right] * 4, "y")
    d, c1 = lax.optimization_barrier(tuple(cores(right)))
    changed = product(one, jnp.where(core == 1, d, c1))
    changed += dot(two, jnp.where(core == 1, c1, d))
    trail = (jnp.where(j >= 16, a, zeros).astype(F32) - changed).astype(BF)
    row0 = jnp.where(in0, a, r)
    row1 = jnp.where(j < 16, w, r1)
    return jnp.where(y > 0, trail, jnp.where(core == 0, row0, row1))


def solution(mesh):
    fine = Mesh(mesh.devices.reshape(4, 2, 4, 16), ("y", "core", "x", "z"))
    placed = (
        P(("y", "core"), ("x", "z")),
        P(None, ("y", "core"), None),
        P(None, ("y", "core"), None),
    )
    return jax.shard_map(
        shards, mesh=fine, in_specs=placed, out_specs=placed[0], check_vma=False
    )
```

```python
import jax
import jax.numpy as jnp
from jax import lax
from jax.sharding import Mesh, PartitionSpec as P

NB = 1024
BF = jnp.bfloat16
F32 = jnp.float32


def dot(a, b):
    return jnp.dot(a, b, preferred_element_type=F32)


def after(value, *others):
    return lax.optimization_barrier((value,) + others)[0]


def from_first(values, axis):
    at = lax.axis_index(axis)
    out = values[0]
    got = [lax.ppermute(v, axis, [(0, k)]) for k, v in enumerate(values) if k > 0]
    for k, v in enumerate(got):
        out = jnp.where(at == k + 1, v, out)
    return out


def copies(piece, count):
    return jnp.broadcast_to(piece[None], (count,) + piece.shape)


def cores(value):
    return lax.all_gather(value, "core", axis=0)


def shards(a, lower, upper):
    y = lax.axis_index("y")
    core = lax.axis_index("core")
    x = lax.axis_index("x")
    z = lax.axis_index("z")
    j = x * 16 + z
    in0 = j < 8
    in1 = (j >= 8) & (j < 16)
    zeros = jnp.zeros_like(a)

    share = from_first([a[256 * k : 256 * (k + 1)] for k in range(4)], "x")

    inverses = jnp.stack([lower, upper], axis=1)
    kept = lax.dynamic_index_in_dim(inverses, core, 0, False)
    given = lax.dynamic_index_in_dim(inverses, 1 - core, 0, False)
    taken = lax.ppermute(given, "core", [(0, 1), (1, 0)])
    pair = jnp.where(core == 0, jnp.stack([kept, taken], 1), jnp.stack([taken, kept], 1))
    pair = after(pair, share)
    parts = [pair] + [lax.ppermute(pair, "y", [(k, 0)]) for k in range(1, 4)]

    fours = [[k, k + 4, k + 8, k + 12] for k in range(4)]
    own = lax.all_to_all(copies(share, 4), "z", 0, 0, axis_index_groups=fours)

    def from_z(value, distance):
        return lax.ppermute(value, "z", [((k + distance) % 16, k) for k in range(16)])

    plus, minus = from_z(own, 1), from_z(own, -1)
    two = lax.ppermute(own, "z", [((k + 2 - 4 * (k % 2)) % 16, k) for k in range(16)])
    along = jnp.concatenate([own, plus, two, minus, own, plus, two])
    along = lax.dynamic_slice_in_dim(along, (4 - z % 4) % 4 * 4, 16, 0).reshape(4, 4, 256, 128)

    def half(which):
        blocks = lax.dynamic_slice_in_dim(along, 2 * which, 2, 1)
        return blocks.transpose(1, 0, 2, 3).reshape(8, 256, 128)

    sent = copies(half(1 - core), 4)
    one = lax.all_to_all(sent, "x", 0, 0)

    inv_l, inv_u = (jnp.concatenate([part[m].reshape(256, NB) for part in parts]) for m in range(2))
    inv_l, inv_u = lax.optimization_barrier((inv_l, inv_u))

    def times(inverse, right):
        return dot(inverse, right).astype(BF)

    r = times(inv_l, a)
    start = jnp.clip(j * 128 - core * NB, 0, NB - 128)
    u_cols = lax.dynamic_slice_in_dim(inv_u, start, 128, 1)
    c0 = jnp.where(in0, -u_cols, times(inv_u, r))
    base = lax.optimization_barrier(jnp.where(in1, zeros, c0))
    c0x = cores(c0)[0]

    def product(left, right):
        right = right.reshape(8, 128, 128)
        return jnp.einsum("xzrk,zkn->xrn", left, right, preferred_element_type=F32).reshape(NB, 128)

    w = (jnp.where(in0, zeros, a).astype(F32) - product(one, c0x)).astype(BF)
    r1 = times(inv_l, w)
    c1 = jnp.where(in0, zeros, jnp.where(in1, -u_cols, times(inv_u, r1)))
    c1 = cores(c1)[1]
    t = lax.optimization_barrier(product(one, c1).astype(BF))
    s = lax.optimization_barrier(times(inv_l, t))
    d = (base.astype(F32) - dot(inv_u, s)).astype(BF)
    right = jnp.where(core == 0, d, c1)
    late = after(half(core), r).transpose(1, 0, 2).reshape(256, NB)

    def from_x(value, distance):
        planes = [(4 * p + (k + distance) % 4, 4 * p + k) for p in range(1, 4) for k in range(4)]
        return lax.ppermute(value, ("y", "x"), planes)

    ahead, behind = from_x(late, 1), from_x(late, -1)
    across = jnp.concatenate([from_x(after(ahead[:128], right), 1), from_x(after(behind[128:], right), -1)])
    two = jnp.concatenate([late, ahead, across, behind, late, ahead, across])
    two = lax.dynamic_slice_in_dim(two, (4 - x) % 4 * 256, NB, 0)
    right = from_first([right] * 4, "y")
    d, c1 = lax.optimization_barrier(tuple(cores(right)))
    changed = product(one, jnp.where(core == 1, d, c1))
    changed += dot(two, jnp.where(core == 1, c1, d))
    trail = (jnp.where(j >= 16, a, zeros).astype(F32) - changed).astype(BF)
    row0 = jnp.where(in0, a, r)
    row1 = jnp.where(j < 16, w, r1)
    return jnp.where(y > 0, trail, jnp.where(core == 0, row0, row1))


def solution(mesh):
    fine = Mesh(mesh.devices.reshape(4, 2, 4, 16), ("y", "core", "x", "z"))
    placed = (
        P(("y", "core"), ("x", "z")),
        P(None, ("y", "core"), None),
        P(None, ("y", "core"), None),
    )
    return jax.shard_map(
        shards, mesh=fine, in_specs=placed, out_specs=placed[0], check_vma=False
    )
```

```python
import jax
import jax.numpy as jnp
from jax import lax
from jax.sharding import Mesh, PartitionSpec as P

NB = 1024
BF = jnp.bfloat16
F32 = jnp.float32


def dot(a, b):
    return jnp.dot(a, b, preferred_element_type=F32)


def after(value, *others):
    return lax.optimization_barrier((value,) + others)[0]


def from_first(values, axis):
    at = lax.axis_index(axis)
    out = values[0]
    got = {k: lax.ppermute(values[k], axis, [(0, k)]) for k in (3, 1, 2)}
    for k in (3, 1, 2):
        out = jnp.where(at == k, got[k], out)
    return out


def copies(piece, count):
    return jnp.broadcast_to(piece[None], (count,) + piece.shape)


def cores(value):
    return lax.all_gather(value, "core", axis=0)


def shards(a, lower, upper):
    y = lax.axis_index("y")
    core = lax.axis_index("core")
    x = lax.axis_index("x")
    z = lax.axis_index("z")
    j = x * 16 + z
    in0 = j < 8
    in1 = (j >= 8) & (j < 16)
    zeros = jnp.zeros_like(a)

    share = from_first([a[256 * k : 256 * (k + 1)] for k in range(4)], "x")

    inverses = jnp.stack([lower, upper], axis=1)
    kept = lax.dynamic_index_in_dim(inverses, core, 0, False)
    given = lax.dynamic_index_in_dim(inverses, 1 - core, 0, False)
    taken = lax.ppermute(given, "core", [(0, 1), (1, 0)])
    pair = jnp.where(core == 0, jnp.stack([kept, taken], 1), jnp.stack([taken, kept], 1))
    pair = after(pair, share)
    parts = [pair] + [lax.ppermute(pair, "y", [(k, 0)]) for k in range(1, 4)]

    fours = [[k, k + 4, k + 8, k + 12] for k in range(4)]
    own = lax.all_to_all(copies(share, 4), "z", 0, 0, axis_index_groups=fours)

    def from_z(value, distance):
        return lax.ppermute(value, "z", [((k + distance) % 16, k) for k in range(16)])

    plus, minus = from_z(own, 1), from_z(own, -1)
    two = lax.ppermute(own, "z", [((k + 2 - 4 * (k % 2)) % 16, k) for k in range(16)])
    along = jnp.concatenate([own, plus, two, minus, own, plus, two])
    along = lax.dynamic_slice_in_dim(along, (4 - z % 4) % 4 * 4, 16, 0).reshape(4, 4, 256, 128)

    def half(which):
        blocks = lax.dynamic_slice_in_dim(along, 2 * which, 2, 1)
        return blocks.transpose(1, 0, 2, 3).reshape(8, 256, 128)

    sent = copies(half(1 - core), 4)
    one = lax.all_to_all(sent, "x", 0, 0)

    inv_l, inv_u = (jnp.concatenate([part[m].reshape(256, NB) for part in parts]) for m in range(2))
    inv_l, inv_u = lax.optimization_barrier((inv_l, inv_u))

    def times(inverse, right):
        return dot(inverse, right).astype(BF)

    r = times(inv_l, a)
    start = jnp.clip(j * 128 - core * NB, 0, NB - 128)
    u_cols = lax.dynamic_slice_in_dim(inv_u, start, 128, 1)
    minus_u = lax.optimization_barrier(-u_cols)
    c0 = jnp.where(in0, minus_u, times(inv_u, r))
    base = lax.optimization_barrier(jnp.where(in1, zeros, c0))
    c0x = cores(c0)[0]

    def product(left, right):
        right = right.reshape(8, 128, 128)
        return jnp.einsum("xzrk,zkn->xrn", left, right, preferred_element_type=F32).reshape(NB, 128)

    w = (jnp.where(in0, zeros, a).astype(F32) - product(one, c0x)).astype(BF)
    r1 = times(inv_l, w)
    c1 = jnp.where(in0, zeros, jnp.where(in1, minus_u, times(inv_u, r1)))
    c1 = cores(c1)[1]
    t = lax.optimization_barrier(product(one, c1).astype(BF))
    s = lax.optimization_barrier(times(inv_l, t))
    d = (base.astype(F32) - dot(inv_u, s)).astype(BF)
    right = jnp.where(core == 0, d, c1)
    late = after(half(core), c0).transpose(1, 0, 2).reshape(256, NB)

    def from_x(value, distance):
        planes = [(4 * p + (k + distance) % 4, 4 * p + k) for p in range(1, 4) for k in range(4)]
        return lax.ppermute(value, ("y", "x"), planes)

    ahead, behind = from_x(late, 1), from_x(late, -1)
    across = jnp.concatenate([from_x(after(ahead[:128], right), 1), from_x(after(behind[128:], right), -1)])
    two = jnp.concatenate([late, ahead, across, behind, late, ahead, across])
    two = lax.dynamic_slice_in_dim(two, (4 - x) % 4 * 256, NB, 0)
    right = from_first([right] * 4, "y")
    d, c1 = lax.optimization_barrier(tuple(cores(right)))
    changed = product(one, jnp.where(core == 1, d, c1))
    changed += dot(two, jnp.where(core == 1, c1, d))
    trail = (jnp.where(j >= 16, a, zeros).astype(F32) - changed).astype(BF)
    row0 = jnp.where(in0, a, r)
    row1 = jnp.where(j < 16, w, r1)
    return jnp.where(y > 0, trail, jnp.where(core == 0, row0, row1))


def solution(mesh):
    fine = Mesh(mesh.devices.reshape(4, 2, 4, 16), ("y", "core", "x", "z"))
    placed = (
        P(("y", "core"), ("x", "z")),
        P(None, ("y", "core"), None),
        P(None, ("y", "core"), None),
    )
    return jax.shard_map(
        shards, mesh=fine, in_specs=placed, out_specs=placed[0], check_vma=False
    )
```

```python
import jax
import jax.numpy as jnp
from jax import lax
from jax.sharding import Mesh, PartitionSpec as P

NB = 1024
BF = jnp.bfloat16
F32 = jnp.float32


def dot(a, b):
    return jnp.dot(a, b, preferred_element_type=F32)


def after(value, *others):
    return lax.optimization_barrier((value,) + others)[0]


def from_first(values, axis):
    at = lax.axis_index(axis)
    out = values[0]
    got = {k: lax.ppermute(values[k], axis, [(0, k)]) for k in (3, 1, 2)}
    for k in (3, 1, 2):
        out = jnp.where(at == k, got[k], out)
    return out


def copies(piece, count):
    return jnp.broadcast_to(piece[None], (count,) + piece.shape)


def cores(value):
    return lax.all_gather(value, "core", axis=0)


def shards(a, lower, upper):
    y = lax.axis_index("y")
    core = lax.axis_index("core")
    x = lax.axis_index("x")
    z = lax.axis_index("z")
    j = x * 16 + z
    in0 = j < 8
    in1 = (j >= 8) & (j < 16)
    zeros = jnp.zeros_like(a)

    share = from_first([a[256 * k : 256 * (k + 1)] for k in range(4)], "x")

    inverses = jnp.stack([lower, upper], axis=1)
    kept = lax.dynamic_index_in_dim(inverses, core, 0, False)
    given = lax.dynamic_index_in_dim(inverses, 1 - core, 0, False)
    taken = lax.ppermute(given, "core", [(0, 1), (1, 0)])
    pair = jnp.where(core == 0, jnp.stack([kept, taken], 1), jnp.stack([taken, kept], 1))
    pair = after(pair, share)
    parts = [pair] + [lax.ppermute(pair, "y", [(k, 0)]) for k in range(1, 4)]

    fours = [[k, k + 4, k + 8, k + 12] for k in range(4)]
    own = lax.all_to_all(copies(share, 4), "z", 0, 0, axis_index_groups=fours)

    def from_z(value, distance):
        return lax.ppermute(value, "z", [((k + distance) % 16, k) for k in range(16)])

    plus, minus = from_z(own, 1), from_z(own, -1)
    two = lax.ppermute(own, "z", [((k + 2 - 4 * (k % 2)) % 16, k) for k in range(16)])
    along = jnp.concatenate([own, plus, two, minus, own, plus, two])
    along = lax.dynamic_slice_in_dim(along, (4 - z % 4) % 4 * 4, 16, 0).reshape(4, 4, 256, 128)

    def half(which):
        blocks = lax.dynamic_slice_in_dim(along, 2 * which, 2, 1)
        return blocks.transpose(1, 0, 2, 3).reshape(8, 256, 128)

    sent = copies(half(1 - core), 4)
    one = lax.all_to_all(sent, "x", 0, 0)

    inv_l, inv_u = (jnp.concatenate([part[m].reshape(256, NB) for part in parts]) for m in range(2))
    inv_l, inv_u = lax.optimization_barrier((inv_l, inv_u))

    def times(inverse, right):
        return dot(inverse, right).astype(BF)

    r = times(inv_l, a)
    start = jnp.clip(j * 128 - core * NB, 0, NB - 128)
    u_cols = lax.dynamic_slice_in_dim(inv_u, start, 128, 1)
    minus_u = lax.optimization_barrier(-u_cols)
    c0 = jnp.where(in0, minus_u, times(inv_u, r))
    base = lax.optimization_barrier(jnp.where(in1, zeros, c0))
    c0x = cores(c0)[0]
    kept_half, c0x = lax.optimization_barrier((half(core), c0x))

    def product(left, right):
        right = right.reshape(8, 128, 128)
        return jnp.einsum("xzrk,zkn->xrn", left, right, preferred_element_type=F32).reshape(NB, 128)

    w = (jnp.where(in0, zeros, a).astype(F32) - product(one, c0x)).astype(BF)
    r1 = times(inv_l, w)
    c1 = jnp.where(in0, zeros, jnp.where(in1, minus_u, times(inv_u, r1)))
    c1 = cores(c1)[1]
    t = lax.optimization_barrier(product(one, c1).astype(BF))
    s = lax.optimization_barrier(times(inv_l, t))
    d = (base.astype(F32) - dot(inv_u, s)).astype(BF)
    right = jnp.where(core == 0, d, c1)
    late = kept_half.transpose(1, 0, 2).reshape(256, NB)

    def from_x(value, distance):
        planes = [(4 * p + (k + distance) % 4, 4 * p + k) for p in range(1, 4) for k in range(4)]
        return lax.ppermute(value, ("y", "x"), planes)

    ahead, behind = from_x(late, 1), from_x(late, -1)
    across = jnp.concatenate([from_x(after(ahead[:128], right), 1), from_x(after(behind[128:], right), -1)])
    two = jnp.concatenate([late, ahead, across, behind, late, ahead, across])
    two = lax.dynamic_slice_in_dim(two, (4 - x) % 4 * 256, NB, 0)
    right = from_first([right] * 4, "y")
    d, c1 = lax.optimization_barrier(tuple(cores(right)))
    changed = product(one, jnp.where(core == 1, d, c1))
    changed += dot(two, jnp.where(core == 1, c1, d))
    trail = (jnp.where(j >= 16, a, zeros).astype(F32) - changed).astype(BF)
    row0 = jnp.where(in0, a, r)
    row1 = jnp.where(j < 16, w, r1)
    return jnp.where(y > 0, trail, jnp.where(core == 0, row0, row1))


def solution(mesh):
    fine = Mesh(mesh.devices.reshape(4, 2, 4, 16), ("y", "core", "x", "z"))
    placed = (
        P(("y", "core"), ("x", "z")),
        P(None, ("y", "core"), None),
        P(None, ("y", "core"), None),
    )
    return jax.shard_map(
        shards, mesh=fine, in_specs=placed, out_specs=placed[0], check_vma=False
    )
```

```python
import jax
import jax.numpy as jnp
from jax import lax
from jax.sharding import Mesh, PartitionSpec as P

NB = 1024
BF = jnp.bfloat16
F32 = jnp.float32


def dot(a, b):
    return jnp.dot(a, b, preferred_element_type=F32)


def after(value, *others):
    return lax.optimization_barrier((value,) + others)[0]


def from_first(values, axis):
    at = lax.axis_index(axis)
    out = values[0]
    got = {k: lax.ppermute(values[k], axis, [(0, k)]) for k in (3, 1, 2)}
    for k in (3, 1, 2):
        out = jnp.where(at == k, got[k], out)
    return out


def copies(piece, count):
    return jnp.broadcast_to(piece[None], (count,) + piece.shape)


def cores(value):
    return lax.all_gather(value, "core", axis=0)


def shards(a, lower, upper):
    y = lax.axis_index("y")
    core = lax.axis_index("core")
    x = lax.axis_index("x")
    z = lax.axis_index("z")
    j = x * 16 + z
    in0 = j < 8
    in1 = (j >= 8) & (j < 16)
    zeros = jnp.zeros_like(a)

    share = from_first([a[256 * k : 256 * (k + 1)] for k in range(4)], "x")

    inverses = jnp.stack([lower, upper], axis=1)
    kept = lax.dynamic_index_in_dim(inverses, core, 0, False)
    given = lax.dynamic_index_in_dim(inverses, 1 - core, 0, False)
    taken = lax.ppermute(given, "core", [(0, 1), (1, 0)])
    pair = jnp.where(core == 0, jnp.stack([kept, taken], 1), jnp.stack([taken, kept], 1))
    pair = after(pair, share)
    parts = [pair] + [lax.ppermute(pair, "y", [(k, 0)]) for k in range(1, 4)]

    fours = [[k, k + 4, k + 8, k + 12] for k in range(4)]
    own = lax.all_to_all(copies(share, 4), "z", 0, 0, axis_index_groups=fours)

    def from_z(value, distance):
        return lax.ppermute(value, "z", [((k + distance) % 16, k) for k in range(16)])

    plus, minus = from_z(own, 1), from_z(own, -1)
    two = lax.ppermute(own, "z", [((k + 2 - 4 * (k % 2)) % 16, k) for k in range(16)])
    along = jnp.concatenate([two, minus, own, plus, two, minus, own])
    along = lax.dynamic_slice_in_dim(along, (6 - z % 4) % 4 * 4, 16, 0).reshape(4, 4, 256, 128)

    def half(which):
        blocks = lax.dynamic_slice_in_dim(along, 2 * which, 2, 1)
        return blocks.transpose(1, 0, 2, 3).reshape(8, 256, 128)

    sent = copies(half(1 - core), 4)
    one = lax.all_to_all(sent, "x", 0, 0)

    inv_l, inv_u = (jnp.concatenate([part[m].reshape(256, NB) for part in parts]) for m in range(2))
    inv_l, inv_u = lax.optimization_barrier((inv_l, inv_u))

    def times(inverse, right):
        return dot(inverse, right).astype(BF)

    r = times(inv_l, a)
    start = jnp.clip(j * 128 - core * NB, 0, NB - 128)
    u_cols = lax.dynamic_slice_in_dim(inv_u, start, 128, 1)
    minus_u = lax.optimization_barrier(-u_cols)
    c0 = jnp.where(in0, minus_u, times(inv_u, r))
    base = lax.optimization_barrier(jnp.where(in1, zeros, c0))
    c0x = cores(c0)[0]
    kept_half, c0x = lax.optimization_barrier((half(core), c0x))

    def product(left, right):
        right = right.reshape(8, 128, 128)
        return jnp.einsum("xzrk,zkn->xrn", left, right, preferred_element_type=F32).reshape(NB, 128)

    w = (jnp.where(in0, zeros, a).astype(F32) - product(one, c0x)).astype(BF)
    r1 = times(inv_l, w)
    c1 = jnp.where(in0, zeros, jnp.where(in1, minus_u, times(inv_u, r1)))
    c1 = cores(c1)[1]
    t = lax.optimization_barrier(product(one, c1).astype(BF))
    s = lax.optimization_barrier(times(inv_l, t))
    d = (base.astype(F32) - dot(inv_u, s)).astype(BF)
    right = jnp.where(core == 0, d, c1)
    late = kept_half.transpose(1, 0, 2).reshape(256, NB)

    def from_x(value, distance):
        planes = [(4 * p + (k + distance) % 4, 4 * p + k) for p in range(1, 4) for k in range(4)]
        return lax.ppermute(value, ("y", "x"), planes)

    ahead, behind = from_x(late, 1), from_x(late, -1)
    across = jnp.concatenate([from_x(after(ahead[:128], right), 1), from_x(after(behind[128:], right), -1)])
    two = jnp.concatenate([late, ahead, across, behind, late, ahead, across])
    two = lax.dynamic_slice_in_dim(two, (4 - x) % 4 * 256, NB, 0)
    right = from_first([right] * 4, "y")
    changed = dot(two, right) + product(one, lax.ppermute(right, "core", [(0, 1), (1, 0)]))
    trail = (jnp.where(j >= 16, a, zeros).astype(F32) - changed).astype(BF)
    row0 = jnp.where(in0, a, r)
    row1 = jnp.where(j < 16, w, r1)
    return jnp.where(y > 0, trail, jnp.where(core == 0, row0, row1))


def solution(mesh):
    fine = Mesh(mesh.devices.reshape(4, 2, 4, 16), ("y", "core", "x", "z"))
    placed = (
        P(("y", "core"), ("x", "z")),
        P(None, ("y", "core"), None),
        P(None, ("y", "core"), None),
    )
    return jax.shard_map(
        shards, mesh=fine, in_specs=placed, out_specs=placed[0], check_vma=False
    )
```

```python
import jax
import jax.numpy as jnp
from jax import lax
from jax.sharding import Mesh, PartitionSpec as P

NB = 1024
BF = jnp.bfloat16
F32 = jnp.float32


def dot(a, b):
    return jnp.dot(a, b, preferred_element_type=F32)


def after(value, *others):
    return lax.optimization_barrier((value,) + others)[0]


def from_first(values, axis):
    at = lax.axis_index(axis)
    out = values[0]
    got = {k: lax.ppermute(values[k], axis, [(0, k)]) for k in (3, 1, 2)}
    for k in (3, 1, 2):
        out = jnp.where(at == k, got[k], out)
    return out


def copies(piece, count):
    return jnp.broadcast_to(piece[None], (count,) + piece.shape)


def cores(value):
    return lax.all_gather(value, "core", axis=0)


def shards(a, lower, upper):
    y = lax.axis_index("y")
    core = lax.axis_index("core")
    x = lax.axis_index("x")
    z = lax.axis_index("z")
    j = x * 16 + z
    in0 = j < 8
    in1 = (j >= 8) & (j < 16)
    zeros = jnp.zeros_like(a)

    share = from_first([a[256 * k : 256 * (k + 1)] for k in range(4)], "x")

    inverses = jnp.stack([lower, upper], axis=1)
    kept = lax.dynamic_index_in_dim(inverses, core, 0, False)
    given = lax.dynamic_index_in_dim(inverses, 1 - core, 0, False)
    taken = lax.ppermute(given, "core", [(0, 1), (1, 0)])
    pair = jnp.where(core == 0, jnp.stack([kept, taken], 1), jnp.stack([taken, kept], 1))
    pair = after(pair, share)
    parts = [pair] + [lax.ppermute(pair, "y", [(k, 0)]) for k in range(1, 4)]

    fours = [[k, k + 4, k + 8, k + 12] for k in range(4)]
    own = lax.all_to_all(copies(share, 4), "z", 0, 0, axis_index_groups=fours)

    def from_z(value, distance):
        return lax.ppermute(value, "z", [((k + distance) % 16, k) for k in range(16)])

    plus, minus = from_z(own, 1), from_z(own, -1)
    two = lax.ppermute(own, "z", [((k + 2 - 4 * (k % 2)) % 16, k) for k in range(16)])
    along = jnp.concatenate([two, minus, own, plus, two, minus, own])
    along = lax.dynamic_slice_in_dim(along, (6 - z % 4) % 4 * 4, 16, 0).reshape(4, 4, 256, 128)

    def half(which):
        blocks = lax.dynamic_slice_in_dim(along, 2 * which, 2, 1)
        return blocks.transpose(1, 0, 2, 3).reshape(8, 256, 128)

    sent = copies(half(1 - core), 4)
    one = lax.all_to_all(sent, "x", 0, 0)

    inv_l, inv_u = (jnp.concatenate([part[m].reshape(256, NB) for part in parts]) for m in range(2))
    inv_l, inv_u = lax.optimization_barrier((inv_l, inv_u))

    def times(inverse, right):
        return dot(inverse, right).astype(BF)

    r = times(inv_l, a)
    start = jnp.clip(j * 128 - core * NB, 0, NB - 128)
    u_cols = lax.dynamic_slice_in_dim(inv_u, start, 128, 1)
    minus_u = lax.optimization_barrier(-u_cols)
    c0 = jnp.where(in0, minus_u, times(inv_u, r))
    base = lax.optimization_barrier(jnp.where(in1, zeros, c0))
    c0x = cores(c0)[0]
    kept_half, c0x = lax.optimization_barrier((half(core), c0x))

    def product(left, right):
        right = right.reshape(8, 128, 128)
        return jnp.einsum("xzrk,zkn->xrn", left, right, preferred_element_type=F32).reshape(NB, 128)

    w = (jnp.where(in0, zeros, a).astype(F32) - product(one, c0x)).astype(BF)
    r1 = times(inv_l, w)
    c1 = jnp.where(in0, zeros, jnp.where(in1, minus_u, times(inv_u, r1)))
    c1x = lax.ppermute(c1, ("y", "core"), [(1, 0)])
    t = lax.optimization_barrier(product(one, c1x).astype(BF))
    s = lax.optimization_barrier(times(inv_l, t))
    d = (base.astype(F32) - dot(inv_u, s)).astype(BF)
    right = jnp.where(core == 0, d, c1)
    late = kept_half.transpose(1, 0, 2).reshape(256, NB)

    def from_x(value, distance):
        planes = [(4 * p + (k + distance) % 4, 4 * p + k) for p in range(1, 4) for k in range(4)]
        return lax.ppermute(value, ("y", "x"), planes)

    ahead, behind = from_x(late, 1), from_x(late, -1)
    across = jnp.concatenate([from_x(after(ahead[:128], right), 1), from_x(after(behind[128:], right), -1)])
    two = jnp.concatenate([late, ahead, across, behind, late, ahead, across])
    two = lax.dynamic_slice_in_dim(two, (4 - x) % 4 * 256, NB, 0)
    right = from_first([right] * 4, "y")
    changed = dot(two, right) + product(one, lax.ppermute(right, "core", [(0, 1), (1, 0)]))
    trail = (jnp.where(j >= 16, a, zeros).astype(F32) - changed).astype(BF)
    row0 = jnp.where(in0, a, r)
    row1 = jnp.where(j < 16, w, r1)
    return jnp.where(y > 0, trail, jnp.where(core == 0, row0, row1))


def solution(mesh):
    fine = Mesh(mesh.devices.reshape(4, 2, 4, 16), ("y", "core", "x", "z"))
    placed = (
        P(("y", "core"), ("x", "z")),
        P(None, ("y", "core"), None),
        P(None, ("y", "core"), None),
    )
    return jax.shard_map(
        shards, mesh=fine, in_specs=placed, out_specs=placed[0], check_vma=False
    )
```

```python
import jax
import jax.numpy as jnp
from jax import lax
from jax.sharding import Mesh, PartitionSpec as P

NB = 1024
BF = jnp.bfloat16
F32 = jnp.float32


def dot(a, b):
    return jnp.dot(a, b, preferred_element_type=F32)


def after(value, *others):
    return lax.optimization_barrier((value,) + others)[0]


def from_first(values, axis, order=(3, 1, 2)):
    at = lax.axis_index(axis)
    out = values[0]
    got = {k: lax.ppermute(values[k], axis, [(0, k)]) for k in (3, 1, 2)}
    for k in order:
        out = jnp.where(at == k, got[k], out)
    return out


def copies(piece, count):
    return jnp.broadcast_to(piece[None], (count,) + piece.shape)


def cores(value):
    return lax.all_gather(value, "core", axis=0)


def shards(a, lower, upper):
    y = lax.axis_index("y")
    core = lax.axis_index("core")
    x = lax.axis_index("x")
    z = lax.axis_index("z")
    j = x * 16 + z
    in0 = j < 8
    in1 = (j >= 8) & (j < 16)
    zeros = jnp.zeros_like(a)

    share = from_first([a[256 * k : 256 * (k + 1)] for k in range(4)], "x")

    inverses = jnp.stack([lower, upper], axis=1)
    kept = lax.dynamic_index_in_dim(inverses, core, 0, False)
    given = lax.dynamic_index_in_dim(inverses, 1 - core, 0, False)
    taken = lax.ppermute(given, "core", [(0, 1), (1, 0)])
    pair = jnp.where(core == 0, jnp.stack([kept, taken], 1), jnp.stack([taken, kept], 1))
    pair = after(pair, share)
    parts = [pair] + [lax.ppermute(pair, "y", [(k, 0)]) for k in range(1, 4)]

    fours = [[k, k + 4, k + 8, k + 12] for k in range(4)]
    own = lax.all_to_all(copies(share, 4), "z", 0, 0, axis_index_groups=fours)

    def from_z(value, distance):
        return lax.ppermute(value, "z", [((k + distance) % 16, k) for k in range(16)])

    plus, minus = from_z(own, 1), from_z(own, -1)
    two = lax.ppermute(own, "z", [((k + 2 - 4 * (k % 2)) % 16, k) for k in range(16)])
    along = jnp.concatenate([two, minus, own, plus, two, minus, own])
    along = lax.dynamic_slice_in_dim(along, (6 - z % 4) % 4 * 4, 16, 0).reshape(4, 4, 256, 128)

    def half(which):
        blocks = lax.dynamic_slice_in_dim(along, 2 * which, 2, 1)
        return blocks.transpose(1, 0, 2, 3).reshape(8, 256, 128)

    sent = copies(half(1 - core), 4)
    one = lax.all_to_all(sent, "x", 0, 0)

    inv_l, inv_u = (jnp.concatenate([part[m].reshape(256, NB) for part in parts]) for m in range(2))
    inv_l, inv_u = lax.optimization_barrier((inv_l, inv_u))

    def times(inverse, right):
        return dot(inverse, right).astype(BF)

    r = times(inv_l, a)
    start = jnp.clip(j * 128 - core * NB, 0, NB - 128)
    u_cols = lax.dynamic_slice_in_dim(inv_u, start, 128, 1)
    minus_u = lax.optimization_barrier(-u_cols)
    c0 = jnp.where(in0, minus_u, times(inv_u, r))
    base = lax.optimization_barrier(jnp.where(in1, zeros, c0))
    c0x = cores(c0)[0]
    kept_half, c0x = lax.optimization_barrier((half(core), c0x))

    def product(left, right):
        right = right.reshape(8, 128, 128)
        return jnp.einsum("xzrk,zkn->xrn", left, right, preferred_element_type=F32).reshape(NB, 128)

    w = (jnp.where(in0, zeros, a).astype(F32) - product(one, c0x)).astype(BF)
    r1 = times(inv_l, w)
    c1 = jnp.where(in0, zeros, jnp.where(in1, minus_u, times(inv_u, r1)))
    c1 = cores(c1)[1]
    t = lax.optimization_barrier(product(one, c1).astype(BF))
    s = lax.optimization_barrier(times(inv_l, t))
    d = (base.astype(F32) - dot(inv_u, s)).astype(BF)
    right = jnp.where(core == 0, d, c1)
    late = kept_half.transpose(1, 0, 2).reshape(256, NB)

    def from_x(value, distance):
        planes = [(4 * p + (k + distance) % 4, 4 * p + k) for p in range(1, 4) for k in range(4)]
        return lax.ppermute(value, ("y", "x"), planes)

    ahead, behind = from_x(late, 1), from_x(late, -1)
    across = jnp.concatenate([from_x(after(ahead[:128], right), 1), from_x(after(behind[128:], right), -1)])
    two = jnp.concatenate([late, ahead, across, behind, late, ahead, across])
    two = lax.dynamic_slice_in_dim(two, (4 - x) % 4 * 256, NB, 0)
    right = from_first([right] * 4, "y", (2, 3, 1))
    changed = dot(two, right) + product(one, lax.ppermute(right, "core", [(0, 1), (1, 0)]))
    trail = (jnp.where(j >= 16, a, zeros).astype(F32) - changed).astype(BF)
    row0 = jnp.where(in0, a, r)
    row1 = jnp.where(j < 16, w, r1)
    return jnp.where(y > 0, trail, jnp.where(core == 0, row0, row1))


def solution(mesh):
    fine = Mesh(mesh.devices.reshape(4, 2, 4, 16), ("y", "core", "x", "z"))
    placed = (
        P(("y", "core"), ("x", "z")),
        P(None, ("y", "core"), None),
        P(None, ("y", "core"), None),
    )
    return jax.shard_map(
        shards, mesh=fine, in_specs=placed, out_specs=placed[0], check_vma=False
    )
```
